32 devices in a mesh: row: 4 (over y, core), col: 8 (over z, x).
Axes of the slice: x: 2, y: 2, z: 4, core: 2. Of those that a mesh axis runs over, the one named last changes fastest.
Arguments:
- kernel_panel: float32 [64, 16384], P(None, ('row', 'col')), may hold values from -4 to 16, as said below
- kernel_slab: float32 [16384, 4096], P('row', 'col'), may hold values from -4 to 20, as said below
- targets: float32 [256, 16384], P(None, ('row', 'col')), may hold values from -6 to 6
Outputs:
- updated_slab: float32 [16384, 4096], P('row', 'col')
- solved_targets: float32 [256, 16384], P('col', 'row')
- panel_factor: float32 [64, 16384], P(None, ('row', 'col'))
The draws below stay inside these ranges and needn't reach their ends.
Inputs may be any that keep to these rules, and one draw needn't show every extreme that they name: kernel_panel[:, 0:64] is symmetric and positive definite. `kernel_slab`: rows 0 to 63 equal kernel_panel[:, 16384 - 4096 : 16384]; the last 4096 rows form a symmetric matrix.
All inputs are finite; a program needn't handle non-finite values.
Results may differ from the reference program's by a relative error of at most 0.00018.
Values sent between devices are 32-bit elements; how exact they have to be, the bound alone decides.
A program may use at most 64 MiB of HBM per device.

```python
import math
import jax
import jax.numpy as jnp
from jax import lax

PANEL = 64
SLAB = 4096
TGT = 256
NR = 16384


def panel_core(key):
    keys = jax.random.split(jax.random.fold_in(key, 7), 5)
    jitter = jax.random.uniform(keys[0], (PANEL,), jnp.float32, -0.4, 0.4)
    points = jnp.arange(PANEL, dtype=jnp.float32) + jitter
    length_scale = 3.0
    amplitude = jnp.exp(jax.random.uniform(keys[1], (PANEL,), jnp.float32, 0.0, math.log(2.0)))
    nugget = jnp.exp(jax.random.uniform(keys[4], (PANEL,), jnp.float32, 0.0, math.log(4.0)))
    spacing = (points[:, None] - points[None, :]) / length_scale
    gram = amplitude[:, None] * amplitude[None, :] * jnp.exp(-0.5 * spacing * spacing)
    identity = jnp.eye(PANEL, dtype=jnp.float32)
    corner = gram + identity * nugget[None, :]
    remain = 0.5 * jax.random.truncated_normal(keys[2], -4.0, 4.0, (PANEL, NR - PANEL), jnp.float32)
    return jnp.concatenate([corner, remain], 1)


def draw_kernel_panel(key, part):
    return panel_core(key)


def draw_kernel_slab(key, part):
    keys = jax.random.split(jax.random.fold_in(key, 13), 2)
    base = jax.random.truncated_normal(keys[0], -4.0, 4.0, (NR, SLAB), jnp.float32)
    square = base[NR - SLAB:]
    diag_values = jnp.exp(jax.random.uniform(keys[1], (SLAB,), jnp.float32, math.log(8.0), math.log(16.0)))
    square = 0.5 * (square + square.T) + jnp.eye(SLAB, dtype=jnp.float32) * diag_values[None, :]
    head_rows = panel_core(key)[:, NR - SLAB:]
    return jnp.concatenate([head_rows, base[PANEL:NR - SLAB], square], 0)


def steps_of(key, shape, shards, smallest, high):
    def one(position, shards_of):
        draws = jax.random.uniform(jax.random.fold_in(jax.random.fold_in(key, 6), position), (shards_of,), jnp.float32, smallest / len(shards), high / len(shards))
        return jnp.repeat(jnp.exp(draws), shape[position] // shards_of).reshape((-1,) + (1,) * (len(shape) - position - 1))

    factor_of = one(*shards[0])
    for cut in shards[1:]:
        factor_of = factor_of * one(*cut)
    return factor_of


def centred(stream_key, shape, spread, most, cuts=(), kind=jnp.bfloat16):
    values = jax.random.normal(stream_key, shape, jnp.float32) * spread
    if len(cuts) > 0:
        values = steps_of(stream_key, shape, cuts, -0.22, 0.18) * values
    return jnp.clip(values, min=-most, max=most).astype(kind)


def setup_inputs(seed: int = 0) -> dict:
    seeds = jax.random.split(jax.random.key(seed), 4)
    return {
        "kernel_panel": draw_kernel_panel(jax.random.fold_in(seeds[3], 71), 0),
        "kernel_slab": draw_kernel_slab(jax.random.fold_in(seeds[3], 71), 0),
        "targets": centred(seeds[2], (TGT, NR), 1.0, 6.0, ((1, 32),), jnp.float32),
    }


def lower_solve(factor, values):
    return jax.scipy.linalg.solve_triangular(factor, values, lower=True)

def reference(kernel_panel, kernel_slab, targets):
    lower_factor = jnp.linalg.cholesky(kernel_panel[:, :PANEL])
    panel_factor = lower_solve(lower_factor, kernel_panel)
    slab_factor = panel_factor[:, NR - SLAB:]
    product = lax.dot_general(panel_factor.astype(jnp.float32), slab_factor.astype(jnp.float32), (((0,), (0,)), ((), ())), precision=lax.Precision.HIGHEST, preferred_element_type=jnp.float32)
    update = kernel_slab - product
    updated_slab = jnp.concatenate([slab_factor, update[PANEL:]], 0)
    solved_lead = lower_solve(lower_factor, targets[:, :PANEL].T).T
    result = targets - jnp.dot(solved_lead.astype(jnp.float32), panel_factor.astype(jnp.float32), precision=lax.Precision.HIGHEST, preferred_element_type=jnp.float32)
    solved_targets = jnp.concatenate([solved_lead, result[:, PANEL:]], 1)
    return (updated_slab, solved_targets, panel_factor)
```

```python
import functools

import jax
import jax.numpy as jnp
from jax import lax
from jax.experimental import pallas as pl
from jax.experimental.pallas import tpu as pltpu
from jax.sharding import PartitionSpec as P

MESH = pl.DeviceIdType.MESH
HIGHEST = lax.Precision.HIGHEST
Z_SIZE = 4


def dot(a, b, dims=((1,), (0,)), precision=None):
    return lax.dot_general(a, b, (dims, ((), ())), precision=precision, preferred_element_type=jnp.float32)


def split3(value):
    high = value.astype(jnp.bfloat16)
    rest = value - high.astype(jnp.float32)
    mid = rest.astype(jnp.bfloat16)
    low = (rest - mid.astype(jnp.float32)).astype(jnp.bfloat16)
    return high, mid, low


def inverse_factor(corner):
    size = corner.shape[0]
    rows = lax.broadcasted_iota(jnp.int32, corner.shape, 0)
    lanes = lax.broadcasted_iota(jnp.int32, corner.shape, 1)
    work = jnp.where(lanes < size, corner, jnp.where(lanes == rows + size, 1.0, 0.0))
    for j in range(size):
        pivot = work[j : j + 1, :]
        scaled = pivot * (1.0 / work[j : j + 1, j : j + 1])
        work = work - jnp.where(rows > j, work[:, j : j + 1], 0.0) * scaled
    diagonal = jnp.sum(jnp.where(lanes == rows, work, 0.0), axis=1, keepdims=True)
    return work * (1.0 / jnp.sqrt(diagonal))


def kernel(
    rows_n, cols_n, k_ref, lead_ref, t_ref, s_ref, us_ref, st_ref, pf_ref,
    gp, tg, ks, note, notes, xtp, rhs, yp,
    slab_sem, own_sem, up_sem, down_sem, side_sem, panel_sem, t_send, t_recv, ks_send, ks_recv,
    note_send, note_fwd, note_recv,
):
    row, col = lax.axis_index("row"), lax.axis_index("col")
    size, blk = k_ref.shape
    tgt = tg.shape[1]
    zn = Z_SIZE
    xn = cols_n // zn
    z, x = col // xn, col % xn
    last = rows_n - 1

    def remote(src, dst, send, recv, where):
        return pltpu.make_async_remote_copy(
            src_ref=src, dst_ref=dst, send_sem=send, recv_sem=recv, device_id=where, device_id_type=MESH
        )

    def slab_copy(b):
        part = pl.ds(pl.multiple_of(b * blk, blk), blk)
        return pltpu.make_async_copy(s_ref.at[part], us_ref.at[part], slab_sem.at[b])

    own_target = pltpu.make_async_copy(
        t_ref.at[pl.ds(pl.multiple_of(col * tgt, tgt), tgt)], tg.at[col], own_sem
    )

    barrier = pltpu.get_barrier_semaphore()
    for step in range(1, cols_n):
        pl.semaphore_signal(barrier, inc=1, device_id=(row, lax.rem(col + step, cols_n)), device_id_type=MESH)
    for step in range(1, rows_n):
        pl.semaphore_signal(barrier, inc=1, device_id=(lax.rem(row + step, rows_n), col), device_id_type=MESH)
    own_target.start()
    for b in range(cols_n):
        slab_copy(b).start()
    gp[col] = k_ref[...]
    pl.semaphore_wait(barrier, cols_n - 1 + rows_n - 1)

    def up(zo):
        o = zo * xn + x
        return remote(gp.at[o], gp.at[o], up_sem.at[zo], panel_sem.at[o], (row, col + xn))

    def down(zo):
        o = zo * xn + x
        return remote(gp.at[o], gp.at[o], down_sem.at[zo], panel_sem.at[o], (row, col - xn))

    def side(zo, step):
        o = zo * xn + x
        peer = z * xn + lax.rem(x + step, xn)
        return remote(gp.at[o], gp.at[o], side_sem.at[zo, step - 1], panel_sem.at[o], (row, peer))

    def slab_panel(step):
        return remote(k_ref, ks, ks_send.at[step - 1], ks_recv, (lax.rem(row + step, rows_n), col))

    def target(step):
        peer = lax.rem(col + step, cols_n)
        return remote(
            t_ref.at[pl.ds(pl.multiple_of(peer * tgt, tgt), tgt)], tg.at[col],
            t_send.at[step - 1], t_recv.at[col], (row, peer),
        )

    def note_out(c):
        return remote(notes.at[c], note, note_send.at[c], note_recv, (row, c))

    def note_on(step):
        return remote(note, note, note_fwd.at[step - 1], note_recv, (lax.rem(row + step, rows_n), col))

    @pl.when(z + 1 < zn)
    def _():
        up(z).start()

    @pl.when(z > 0)
    def _():
        down(z).start()

    for step in range(1, xn):
        side(z, step).start()

    @pl.when(row == last)
    def _():
        for step in range(1, rows_n):
            slab_panel(step).start()

    for step in range(1, cols_n):
        target(step).start()

    @pl.when((row == 0) & (col == 0))
    def _():
        done = inverse_factor(k_ref[:, : 2 * size])
        lanes = lax.broadcasted_iota(jnp.int32, done.shape, 1)
        for c in range(cols_n):
            lead = lead_ref[c * tgt : (c + 1) * tgt, :]
            notes[c] = done
            notes[c, :tgt, :] = jnp.where(lanes[:tgt] < size, lead, done[:tgt])
        note[...] = notes[0]
        for c in range(1, cols_n):
            note_out(c).start()

    for d in range(1, zn):
        @pl.when(z - d >= 0)
        def _():
            up(z - d).wait_recv()

            @pl.when(z + 1 < zn)
            def _():
                up(z - d).start()

            for step in range(1, xn):
                side(z - d, step).start()

        @pl.when(z + d < zn)
        def _():
            down(z + d).wait_recv()

            @pl.when(z > 0)
            def _():
                down(z + d).start()

            for step in range(1, xn):
                side(z + d, step).start()

    @pl.when((row > 0) | (col > 0))
    def _():
        remote(note, note, note_fwd.at[0], note_recv, (row, col)).wait_recv()

    @pl.when(row == 0)
    def _():
        for step in range(1, rows_n):
            note_on(step).start()

    @pl.when(row == last)
    def _():
        ks[...] = k_ref[...]

    @pl.when(row != last)
    def _():
        remote(k_ref, ks, ks_send.at[0], ks_recv, (row, col)).wait_recv()

    inverse = note[:, size:]
    wide = jnp.concatenate([note[...]] * 4, axis=0).T[size:, :]
    high, mid, low = split3(wide)
    rhs[...] = jnp.concatenate([high, mid, low, high, mid, high], axis=0)
    pf_ref[...] = dot(inverse, k_ref[...], precision=HIGHEST)
    slab_factor = dot(inverse, ks[...], precision=HIGHEST)
    high, mid, _ = split3(slab_factor)
    yp[...] = jnp.concatenate([high, mid, high, mid], axis=0)

    for step in range(1, xn):
        for zo in range(zn):
            o = zo * xn + lax.rem(x + step, xn)
            remote(gp.at[o], gp.at[o], side_sem.at[0, 0], panel_sem.at[o], (row, col)).wait_recv()

    lanes4 = lax.broadcasted_iota(jnp.int32, (blk, 4 * size), 1)

    def slab_step(b, carry):
        high, mid, low = split3(gp[b])
        lhs = jnp.concatenate([high, high, high, mid, mid, low], axis=0)
        xt = dot(lhs, rhs[...], dims=((0,), (0,)))
        rest = xt - xt.astype(jnp.bfloat16).astype(jnp.float32)
        packed = jnp.where(lanes4 < 2 * size, xt, rest).astype(jnp.bfloat16)
        xtp[b] = packed
        product = dot(packed, yp[...])
        slab_copy(b).wait()
        part = pl.ds(pl.multiple_of(b * blk, blk), blk)
        us_ref[part, :] = us_ref[part, :] - product
        return carry

    lax.fori_loop(0, cols_n, slab_step, 0)

    @pl.when(row == 0)
    def _():
        us_ref[:size, :] = slab_factor

    solved = dot(note[:tgt, :size], wide, precision=HIGHEST)
    lanes = lax.broadcasted_iota(jnp.int32, solved.shape, 1)
    rest = solved - solved.astype(jnp.bfloat16).astype(jnp.float32)
    zp = jnp.where(lax.rem(lanes, 2 * size) < size, solved, rest).astype(jnp.bfloat16)

    own_target.wait()
    for step in range(1, cols_n):
        o = lax.rem(col + step, cols_n)
        remote(t_ref.at[pl.ds(0, tgt)], tg.at[o], t_send.at[0], t_recv.at[o], (row, col)).wait_recv()

    def target_step(b, carry):
        part = pl.ds(pl.multiple_of(b * blk, blk), blk)
        st_ref[:, part] = tg[b] - dot(zp, xtp[b], dims=((1,), (1,)))
        return carry

    lax.fori_loop(0, cols_n, target_step, 0)

    @pl.when(row == 0)
    def _():
        pair = slice(0, 2 * size)
        st_ref[:, pair] = jnp.where(lanes[:, pair] < size, solved[:, pair], st_ref[:, pair])

    for zo in range(zn):
        @pl.when((z >= zo) & (z + 1 < zn))
        def _():
            up(zo).wait_send()

        @pl.when((z <= zo) & (z > 0))
        def _():
            down(zo).wait_send()

        for step in range(1, xn):
            side(zo, step).wait_send()

    for step in range(1, cols_n):
        target(step).wait_send()

    @pl.when(row == last)
    def _():
        for step in range(1, rows_n):
            slab_panel(step).wait_send()

    @pl.when((row == 0) & (col == 0))
    def _():
        for c in range(1, cols_n):
            note_out(c).wait_send()

    @pl.when(row == 0)
    def _():
        for step in range(1, rows_n):
            note_on(step).wait_send()


def body(rows_n, cols_n, kernel_panel, kernel_slab, targets):
    size, blk = kernel_panel.shape
    rows, _ = kernel_slab.shape
    tgt = targets.shape[0] // cols_n
    xn = cols_n // Z_SIZE
    f32 = jnp.float32
    vmem = pl.BlockSpec(memory_space=pltpu.VMEM)
    hbm = pl.BlockSpec(memory_space=pl.ANY)
    dma = pltpu.SemaphoreType.DMA
    us, st, pf = pl.pallas_call(
        functools.partial(kernel, rows_n, cols_n),
        out_shape=OUT((rows, blk), (tgt, rows), (size, blk)),
        in_specs=[vmem, vmem, hbm, hbm],
        out_specs=[vmem] * 3,
        scratch_shapes=[
            pltpu.VMEM((cols_n, size, blk), f32),
            pltpu.VMEM((cols_n, tgt, blk), f32),
            pltpu.VMEM((size, blk), f32),
            pltpu.VMEM((size, 2 * size), f32),
            pltpu.VMEM((cols_n, size, 2 * size), f32),
            pltpu.VMEM((cols_n, blk, 4 * size), jnp.bfloat16),
            pltpu.VMEM((6 * size, 4 * size), jnp.bfloat16),
            pltpu.VMEM((4 * size, blk), jnp.bfloat16),
            dma((cols_n,)), dma, dma((Z_SIZE,)), dma((Z_SIZE,)), dma((Z_SIZE, xn - 1)), dma((cols_n,)),
            dma((cols_n - 1,)), dma((cols_n,)), dma((rows_n - 1,)), dma,
            dma((cols_n,)), dma((rows_n - 1,)), dma,
        ],
        compiler_params=pltpu.CompilerParams(
            collective_id=0, has_side_effects=True, vmem_limit_bytes=36 * 1024 * 1024
        ),
        cost_estimate=pl.CostEstimate(
            flops=2 * rows * blk * 4 * size, bytes_accessed=8 * rows * blk, transcendentals=0
        ),
    )(kernel_panel, targets[:, : 2 * size], targets, kernel_slab)
    return us, st, pf


def OUT(*shapes):
    return [pltpu.VMEM(shape, jnp.float32) for shape in shapes]


def solution(mesh):
    in_specs = (P(None, ("row", "col")), P("row", "col"), P(None, ("row", "col")))
    out_specs = (P("row", "col"), P("col", "row"), P(None, ("row", "col")))
    step = functools.partial(body, mesh.shape["row"], mesh.shape["col"])
    return jax.shard_map(step, mesh=mesh, in_specs=in_specs, out_specs=out_specs, check_vma=False)
```

```python
import functools

import jax
import jax.numpy as jnp
from jax import lax
from jax.experimental import pallas as pl
from jax.experimental.pallas import tpu as pltpu
from jax.sharding import PartitionSpec as P

MESH = pl.DeviceIdType.MESH
HIGHEST = lax.Precision.HIGHEST
Z_SIZE = 4


def dot(a, b, dims=((1,), (0,)), precision=None):
    return lax.dot_general(a, b, (dims, ((), ())), precision=precision, preferred_element_type=jnp.float32)


def split3(value):
    high = value.astype(jnp.bfloat16)
    rest = value - high.astype(jnp.float32)
    mid = rest.astype(jnp.bfloat16)
    low = (rest - mid.astype(jnp.float32)).astype(jnp.bfloat16)
    return high, mid, low


def eliminate_pair(work, j):
    rows = lax.broadcasted_iota(jnp.int32, work.shape, 0)
    first, second = work[j : j + 1, :], work[j + 1 : j + 2, :]
    cross = work[j + 1 : j + 2, j : j + 1]
    scale = 1.0 / work[j : j + 1, j : j + 1]
    ratio = cross * scale
    below = second - ratio * first
    other = 1.0 / (work[j + 1 : j + 2, j + 1 : j + 2] - ratio * cross)
    second_part = below * other
    first_part = first * scale - ratio * second_part
    change = work[:, j : j + 1] * first_part + work[:, j + 1 : j + 2] * second_part
    return jnp.where(rows > j + 1, work - change, jnp.where(rows == j + 1, below, work))


def kernel(
    rows_n, cols_n, k_ref, t_ref, s_ref,
    us_ref, tg, xtp, pf_ref, zp_ref, z_ref, sel_ref,
    gp, ks, note, notes, lead, lhs, rhs, yp,
    slab_sem, own_sem, up_sem, down_sem, side_sem, panel_sem, t_send, t_recv, ks_send, ks_recv,
    note_send, note_fwd, note_recv,
):
    row, col = lax.axis_index("row"), lax.axis_index("col")
    size, blk = k_ref.shape
    tgt = tg.shape[1]
    zn = Z_SIZE
    xn = cols_n // zn
    z, x = col // xn, col % xn
    last = rows_n - 1
    first_device = (row == 0) & (col == 0)

    def remote(src, dst, send, recv, where):
        return pltpu.make_async_remote_copy(
            src_ref=src, dst_ref=dst, send_sem=send, recv_sem=recv, device_id=where, device_id_type=MESH
        )

    def slab_copy(b):
        part = pl.ds(pl.multiple_of(b * blk, blk), blk)
        return pltpu.make_async_copy(s_ref.at[part], us_ref.at[part], slab_sem.at[b])

    own_panel = pltpu.make_async_copy(k_ref, gp.at[col], own_sem.at[0])
    own_target = pltpu.make_async_copy(
        t_ref.at[pl.ds(pl.multiple_of(col * tgt, tgt), tgt)], tg.at[col], own_sem.at[1]
    )
    own_lead = pltpu.make_async_copy(t_ref.at[:, pl.ds(0, 2 * size)], lead, own_sem.at[2])

    barrier = pltpu.get_barrier_semaphore()
    for step in range(1, cols_n):
        pl.semaphore_signal(barrier, inc=1, device_id=(row, lax.rem(col + step, cols_n)), device_id_type=MESH)
    for step in range(1, rows_n):
        pl.semaphore_signal(barrier, inc=1, device_id=(lax.rem(row + step, rows_n), col), device_id_type=MESH)
    own_panel.start()
    own_target.start()

    @pl.when(first_device)
    def _():
        own_lead.start()

    for b in range(cols_n):
        slab_copy(b).start()
    own_panel.wait()
    pl.semaphore_wait(barrier, cols_n - 1 + rows_n - 1)

    def up(zo):
        o = zo * xn + x
        return remote(gp.at[o], gp.at[o], up_sem.at[zo], panel_sem.at[o], (row, col + xn))

    def down(zo):
        o = zo * xn + x
        return remote(gp.at[o], gp.at[o], down_sem.at[zo], panel_sem.at[o], (row, col - xn))

    def side(zo, step):
        o = zo * xn + x
        peer = z * xn + lax.rem(x + step, xn)
        return remote(gp.at[o], gp.at[o], side_sem.at[zo, step - 1], panel_sem.at[o], (row, peer))

    def slab_panel(step):
        return remote(gp.at[col], ks, ks_send.at[step - 1], ks_recv, (lax.rem(row + step, rows_n), col))

    def target(step):
        peer = lax.rem(col + step, cols_n)
        return remote(
            t_ref.at[pl.ds(pl.multiple_of(peer * tgt, tgt), tgt)], tg.at[col],
            t_send.at[step - 1], t_recv.at[col], (row, peer),
        )

    def note_out(c):
        return remote(notes.at[c], note, note_send.at[c], note_recv, (row, c))

    def note_on(step):
        return remote(note, note, note_fwd.at[step - 1], note_recv, (lax.rem(row + step, rows_n), col))

    half = lax.broadcasted_iota(jnp.int32, (blk, 2 * size), 1) < size

    def prepare(o):
        block = gp[o]
        turned = jnp.concatenate([block, block], axis=0).T
        high = turned.astype(jnp.bfloat16).astype(jnp.float32)
        rest = turned - high
        mid = rest.astype(jnp.bfloat16).astype(jnp.float32)
        pair = jnp.where(half, high, mid).astype(jnp.bfloat16)
        other = jnp.where(half, rest - mid, high).astype(jnp.bfloat16)
        lhs[o] = jnp.concatenate([pair, other], axis=1)

    def pass_up(d):
        up(z - d).wait_recv()

        @pl.when(z + 1 < zn)
        def _():
            up(z - d).start()

        for step in range(1, xn):
            side(z - d, step).start()

    def pass_down(d):
        down(z + d).wait_recv()

        @pl.when(z > 0)
        def _():
            down(z + d).start()

        for step in range(1, xn):
            side(z + d, step).start()

    @pl.when(z + 1 < zn)
    def _():
        up(z).start()

    @pl.when(z > 0)
    def _():
        down(z).start()

    for step in range(1, xn):
        side(z, step).start()

    @pl.when(row == last)
    def _():
        for step in range(1, rows_n):
            slab_panel(step).start()

    for step in range(1, cols_n):
        target(step).start()

    @pl.when(first_device)
    def _():
        corner = gp[0, :, : 2 * size]
        rows = lax.broadcasted_iota(jnp.int32, corner.shape, 0)
        lanes = lax.broadcasted_iota(jnp.int32, corner.shape, 1)
        work = jnp.where(lanes < size, corner, jnp.where(lanes == rows + size, 1.0, 0.0))
        for j in range(0, size, 2):
            work = eliminate_pair(work, j)
            if j == size // 2:
                pass_down(1)
            if j == 3 * size // 4:
                pass_down(2)
        diagonal = jnp.sum(jnp.where(lanes == rows, work, 0.0), axis=1, keepdims=True)
        done = work * (1.0 / jnp.sqrt(diagonal))
        own_lead.wait()
        for c in range(cols_n):
            notes[c] = done
            notes[c, :tgt, :] = jnp.where(lanes[:tgt] < size, lead[c * tgt : (c + 1) * tgt, :], done[:tgt])
        for c in range(1, cols_n):
            note_out(c).start()
        note[...] = notes[0]
        for step in range(1, rows_n):
            note_on(step).start()
        pass_down(3)
        prepare(col)
        for d in range(1, zn):
            prepare(col + d * xn)

    @pl.when(jnp.logical_not(first_device))
    def _():
        prepare(col)
        for d in range(1, zn):
            @pl.when(z - d >= 0)
            def _():
                pass_up(d)
                prepare(col - d * xn)

            @pl.when(z + d < zn)
            def _():
                pass_down(d)
                prepare(col + d * xn)

        remote(note, note, note_fwd.at[0], note_recv, (row, col)).wait_recv()

        @pl.when(row == 0)
        def _():
            for step in range(1, rows_n):
                note_on(step).start()

    @pl.when(row == last)
    def _():
        ks[...] = gp[col]

    @pl.when(row != last)
    def _():
        remote(gp.at[col], ks, ks_send.at[0], ks_recv, (row, col)).wait_recv()

    inverse = note[:, size:]
    wide = jnp.concatenate([note[...]] * 4, axis=0).T[size:, :]
    high, mid, low = split3(wide)
    rhs[...] = jnp.concatenate([high, high, high, mid, low, mid], axis=0)
    pf_ref[...] = dot(inverse, gp[col], precision=HIGHEST)
    slab_factor = dot(inverse, ks[...], precision=HIGHEST)
    high, mid, _ = split3(slab_factor)
    yp[...] = jnp.concatenate([high, mid, high, mid], axis=0)
    solved = dot(note[:tgt, :size], wide, precision=HIGHEST)
    lanes = lax.broadcasted_iota(jnp.int32, solved.shape, 1)
    rest = solved - solved.astype(jnp.bfloat16).astype(jnp.float32)
    zp_ref[...] = jnp.where(lax.rem(lanes, 2 * size) < size, solved, rest).astype(jnp.bfloat16)
    z_ref[...] = solved[:, : 2 * size]
    sel_ref[...] = jnp.where((lanes[:, : 2 * size] < size) & (row == 0), 1.0, 0.0)

    lanes4 = lax.broadcasted_iota(jnp.int32, (blk, 4 * size), 1)

    def update(b):
        xt = dot(lhs[b], rhs[: 4 * size]) + dot(lhs[b, :, : 2 * size], rhs[4 * size :])
        rest = xt - xt.astype(jnp.bfloat16).astype(jnp.float32)
        packed = jnp.where(lanes4 < 2 * size, xt, rest).astype(jnp.bfloat16)
        xtp[b] = packed
        slab_copy(b).wait()
        part = pl.ds(pl.multiple_of(b * blk, blk), blk)
        us_ref[part, :] = us_ref[part, :] - dot(packed, yp[...])

    def line_step(zo, carry):
        update(zo * xn + x)
        return carry

    lax.fori_loop(0, zn, line_step, 0)
    for step in range(1, xn):
        def side_step(zo, carry):
            o = zo * xn + lax.rem(x + step, xn)
            remote(gp.at[o], gp.at[o], side_sem.at[0, 0], panel_sem.at[o], (row, col)).wait_recv()
            prepare(o)
            update(o)
            return carry

        lax.fori_loop(0, zn, side_step, 0)

    @pl.when(row == 0)
    def _():
        us_ref[:size, :] = slab_factor

    own_target.wait()
    for step in range(1, cols_n):
        o = lax.rem(col + step, cols_n)
        remote(t_ref.at[pl.ds(0, tgt)], tg.at[o], t_send.at[0], t_recv.at[o], (row, col)).wait_recv()

    for zo in range(zn):
        @pl.when((z >= zo) & (z + 1 < zn))
        def _():
            up(zo).wait_send()

        @pl.when((z <= zo) & (z > 0))
        def _():
            down(zo).wait_send()

        for step in range(1, xn):
            side(zo, step).wait_send()

    for step in range(1, cols_n):
        target(step).wait_send()

    @pl.when(row == last)
    def _():
        for step in range(1, rows_n):
            slab_panel(step).wait_send()

    @pl.when(first_device)
    def _():
        for c in range(1, cols_n):
            note_out(c).wait_send()

    @pl.when(row == 0)
    def _():
        for step in range(1, rows_n):
            note_on(step).wait_send()


def finish(us_in, tg, xtp, pf_in, zp, z_in, sel, us_out, st_out, pf_out, st, sems):
    count, _, blk = tg.shape
    part_rows = us_in.shape[0] // 4
    copies = []
    for part in range(4):
        rows = pl.ds(part * part_rows, part_rows)
        copies.append(pltpu.make_async_copy(us_in.at[rows], us_out.at[rows], sems.at[part]))
    copies.append(pltpu.make_async_copy(pf_in, pf_out, sems.at[4]))
    for copy in copies:
        copy.start()
    for b in range(count):
        st[:, b * blk : (b + 1) * blk] = tg[b] - dot(zp[...], xtp[b], dims=((1,), (1,)))
    width = z_in.shape[1]
    st[:, :width] = jnp.where(sel[...] > 0.5, z_in[...], st[:, :width])
    copies.append(pltpu.make_async_copy(st, st_out, sems.at[5]))
    copies[-1].start()
    for copy in copies:
        copy.wait()


def body(rows_n, cols_n, kernel_panel, kernel_slab, targets):
    size, blk = kernel_panel.shape
    rows, _ = kernel_slab.shape
    tgt = targets.shape[0] // cols_n
    xn = cols_n // Z_SIZE
    f32, bf16 = jnp.float32, jnp.bfloat16
    hbm = pl.BlockSpec(memory_space=pltpu.HBM)
    vmem = pl.BlockSpec(memory_space=pltpu.VMEM)
    dma = pltpu.SemaphoreType.DMA
    held = pl.pallas_call(
        functools.partial(kernel, rows_n, cols_n),
        out_shape=[
            pltpu.VMEM((rows, blk), f32),
            pltpu.VMEM((cols_n, tgt, blk), f32),
            pltpu.VMEM((cols_n, blk, 4 * size), bf16),
            pltpu.VMEM((size, blk), f32),
            pltpu.VMEM((tgt, 4 * size), bf16),
            pltpu.VMEM((tgt, 2 * size), f32),
            pltpu.VMEM((tgt, 2 * size), f32),
        ],
        in_specs=[hbm] * 3,
        out_specs=[vmem] * 7,
        scratch_shapes=[
            pltpu.VMEM((cols_n, size, blk), f32),
            pltpu.VMEM((size, blk), f32),
            pltpu.VMEM((size, 2 * size), f32),
            pltpu.VMEM((cols_n, size, 2 * size), f32),
            pltpu.VMEM((cols_n * tgt, 2 * size), f32),
            pltpu.VMEM((cols_n, blk, 4 * size), bf16),
            pltpu.VMEM((6 * size, 4 * size), bf16),
            pltpu.VMEM((4 * size, blk), bf16),
            dma((cols_n,)), dma((3,)), dma((Z_SIZE,)), dma((Z_SIZE,)), dma((Z_SIZE, xn - 1)), dma((cols_n,)),
            dma((cols_n - 1,)), dma((cols_n,)), dma((rows_n - 1,)), dma,
            dma((cols_n,)), dma((rows_n - 1,)), dma,
        ],
        compiler_params=pltpu.CompilerParams(
            collective_id=0, has_side_effects=True, vmem_limit_bytes=48 * 1024 * 1024
        ),
        cost_estimate=pl.CostEstimate(
            flops=2 * rows * blk * 4 * size, bytes_accessed=4 * rows * blk, transcendentals=0
        ),
    )(kernel_panel, targets, kernel_slab)
    return pl.pallas_call(
        finish,
        out_shape=[
            jax.ShapeDtypeStruct((rows, blk), f32),
            jax.ShapeDtypeStruct((tgt, rows), f32),
            jax.ShapeDtypeStruct((size, blk), f32),
        ],
        in_specs=[vmem] * 7,
        out_specs=[hbm] * 3,
        scratch_shapes=[pltpu.VMEM((tgt, rows), f32), dma((6,))],
        compiler_params=pltpu.CompilerParams(vmem_limit_bytes=36 * 1024 * 1024),
        cost_estimate=pl.CostEstimate(
            flops=2 * rows * tgt * 4 * size, bytes_accessed=4 * rows * blk, transcendentals=0
        ),
    )(*held)


def solution(mesh):
    in_specs = (P(None, ("row", "col")), P("row", "col"), P(None, ("row", "col")))
    out_specs = (P("row", "col"), P("col", "row"), P(None, ("row", "col")))
    step = functools.partial(body, mesh.shape["row"], mesh.shape["col"])
    return jax.shard_map(step, mesh=mesh, in_specs=in_specs, out_specs=out_specs, check_vma=False)
```

```python
import functools

import jax
import jax.numpy as jnp
from jax import lax
from jax.experimental import pallas as pl
from jax.experimental.pallas import tpu as pltpu
from jax.sharding import PartitionSpec as P

MESH = pl.DeviceIdType.MESH
HIGHEST = lax.Precision.HIGHEST
Z_SIZE = 4
PIECES = 2
EARLY = 16


def dot(a, b, dims=((1,), (0,)), precision=None):
    return lax.dot_general(a, b, (dims, ((), ())), precision=precision, preferred_element_type=jnp.float32)


def split3(value):
    high = value.astype(jnp.bfloat16)
    rest = value - high.astype(jnp.float32)
    mid = rest.astype(jnp.bfloat16)
    low = (rest - mid.astype(jnp.float32)).astype(jnp.bfloat16)
    return high, mid, low


def eliminate_pair(work, j):
    rows = lax.broadcasted_iota(jnp.int32, work.shape, 0)
    first, second = work[j : j + 1, :], work[j + 1 : j + 2, :]
    cross = work[j + 1 : j + 2, j : j + 1]
    scale = 1.0 / work[j : j + 1, j : j + 1]
    ratio = cross * scale
    below = second - ratio * first
    other = 1.0 / (work[j + 1 : j + 2, j + 1 : j + 2] - ratio * cross)
    second_part = below * other
    first_part = first * scale - ratio * second_part
    change = work[:, j : j + 1] * first_part + work[:, j + 1 : j + 2] * second_part
    return jnp.where(rows > j + 1, work - change, jnp.where(rows == j + 1, below, work))


def kernel(
    rows_n, cols_n, k_ref, t_ref, s_ref,
    us_ref, tg, xtp, pf_ref, zp_ref, z_ref, sel_ref,
    gp, ks, note, notes, lead, lhs, rhs, yp,
    slab_sem, own_sem, up_sem, down_sem, side_sem, panel_sem, t_send, t_recv, ks_send, ks_recv,
    note_send, note_fwd, note_recv,
):
    row, col = lax.axis_index("row"), lax.axis_index("col")
    size, blk = k_ref.shape
    tgt = tg.shape[1]
    zn = Z_SIZE
    xn = cols_n // zn
    z, x = col // xn, col % xn
    last = rows_n - 1
    first_device = (row == 0) & (col == 0)

    def remote(src, dst, send, recv, where):
        return pltpu.make_async_remote_copy(
            src_ref=src, dst_ref=dst, send_sem=send, recv_sem=recv, device_id=where, device_id_type=MESH
        )

    def slab_copy(b):
        part = pl.ds(pl.multiple_of(b * blk, blk), blk)
        return pltpu.make_async_copy(s_ref.at[part], us_ref.at[part], slab_sem.at[b])

    own_panel = pltpu.make_async_copy(k_ref, gp.at[col], own_sem.at[0])
    own_target = pltpu.make_async_copy(
        t_ref.at[pl.ds(pl.multiple_of(col * tgt, tgt), tgt)], tg.at[col], own_sem.at[1]
    )
    own_lead = pltpu.make_async_copy(t_ref.at[:, pl.ds(0, 2 * size)], lead, own_sem.at[2])

    barrier = pltpu.get_barrier_semaphore()
    for step in range(1, cols_n):
        pl.semaphore_signal(barrier, inc=1, device_id=(row, lax.rem(col + step, cols_n)), device_id_type=MESH)
    for step in range(1, rows_n):
        pl.semaphore_signal(barrier, inc=1, device_id=(lax.rem(row + step, rows_n), col), device_id_type=MESH)
    own_panel.start()
    own_target.start()

    @pl.when(first_device)
    def _():
        own_lead.start()

    for b in range(cols_n):
        slab_copy(b).start()
    own_panel.wait()

    @pl.when(first_device)
    def _():
        corner = gp[0, :, : 2 * size]
        rows = lax.broadcasted_iota(jnp.int32, corner.shape, 0)
        lanes = lax.broadcasted_iota(jnp.int32, corner.shape, 1)
        work = jnp.where(lanes < size, corner, jnp.where(lanes == rows + size, 1.0, 0.0))
        for j in range(0, EARLY, 2):
            work = eliminate_pair(work, j)
        notes[0] = work

    pl.semaphore_wait(barrier, cols_n - 1 + rows_n - 1)

    def piece(o, h):
        return gp.at[o, pl.ds(h * (size // PIECES), size // PIECES)]

    def up(zo, h):
        o = zo * xn + x
        return remote(piece(o, h), piece(o, h), up_sem.at[zo, h], panel_sem.at[o, h], (row, col + xn))

    def down(zo, h):
        o = zo * xn + x
        return remote(piece(o, h), piece(o, h), down_sem.at[zo, h], panel_sem.at[o, h], (row, col - xn))

    def side(zo, step, h):
        o = zo * xn + x
        peer = z * xn + lax.rem(x + step, xn)
        return remote(piece(o, h), piece(o, h), side_sem.at[zo, step - 1, h], panel_sem.at[o, h], (row, peer))

    def slab_panel(step):
        return remote(gp.at[col], ks, ks_send.at[step - 1], ks_recv, (lax.rem(row + step, rows_n), col))

    def target(step):
        peer = lax.rem(col + step, cols_n)
        return remote(
            t_ref.at[pl.ds(pl.multiple_of(peer * tgt, tgt), tgt)], tg.at[col],
            t_send.at[step - 1], t_recv.at[col], (row, peer),
        )

    def note_out(c):
        return remote(notes.at[c], note, note_send.at[c], note_recv, (row, c))

    def note_on(step):
        return remote(note, note, note_fwd.at[step - 1], note_recv, (lax.rem(row + step, rows_n), col))

    half = lax.broadcasted_iota(jnp.int32, (blk, 2 * size), 1) < size

    def prepare(o):
        block = gp[o]
        turned = jnp.concatenate([block, block], axis=0).T
        high = turned.astype(jnp.bfloat16).astype(jnp.float32)
        rest = turned - high
        mid = rest.astype(jnp.bfloat16).astype(jnp.float32)
        pair = jnp.where(half, high, mid).astype(jnp.bfloat16)
        other = jnp.where(half, rest - mid, high).astype(jnp.bfloat16)
        lhs[o] = jnp.concatenate([pair, other], axis=1)

    def pass_up(d):
        for h in range(PIECES):
            up(z - d, h).wait_recv()

            @pl.when(z + 1 < zn)
            def _():
                up(z - d, h).start()

            for step in range(1, xn):
                side(z - d, step, h).start()

    def pass_down(d):
        for h in range(PIECES):
            down(z + d, h).wait_recv()

            @pl.when(z > 0)
            def _():
                down(z + d, h).start()

            for step in range(1, xn):
                side(z + d, step, h).start()

    def take_side(zo):
        for step in range(1, xn):
            o = zo * xn + lax.rem(x + step, xn)
            for h in range(PIECES):
                remote(piece(o, h), piece(o, h), side_sem.at[0, 0, 0], panel_sem.at[o, h], (row, col)).wait_recv()
            prepare(o)

    def take_sides(d):
        if d == 0:
            take_side(z)
        else:
            @pl.when(z - d >= 0)
            def _():
                take_side(z - d)

            @pl.when(z + d < zn)
            def _():
                take_side(z + d)

    for h in range(PIECES):
        @pl.when(z + 1 < zn)
        def _():
            up(z, h).start()

        @pl.when(z > 0)
        def _():
            down(z, h).start()

        for step in range(1, xn):
            side(z, step, h).start()

    @pl.when(row == last)
    def _():
        for step in range(1, rows_n):
            slab_panel(step).start()

    sends = list(range(1, cols_n))
    groups = [sends[g::zn] for g in range(zn)]

    @pl.when(first_device)
    def _():
        for step in sends:
            target(step).start()
        work = notes[0]
        for j in range(EARLY, size, 2):
            work = eliminate_pair(work, j)
        rows = lax.broadcasted_iota(jnp.int32, work.shape, 0)
        lanes = lax.broadcasted_iota(jnp.int32, work.shape, 1)
        diagonal = jnp.sum(jnp.where(lanes == rows, work, 0.0), axis=1, keepdims=True)
        done = work * (1.0 / jnp.sqrt(diagonal))
        own_lead.wait()
        for c in range(cols_n):
            notes[c] = done
            notes[c, :tgt, :] = jnp.where(lanes[:tgt] < size, lead[c * tgt : (c + 1) * tgt, :], done[:tgt])
        for c in range(1, cols_n):
            note_out(c).start()
        note[...] = notes[0]
        for step in range(1, rows_n):
            note_on(step).start()
        for d in range(1, zn):
            pass_down(d)
        prepare(col)
        for d in range(1, zn):
            prepare(col + d * xn)
            take_sides(d - 1)

    @pl.when(jnp.logical_not(first_device))
    def _():
        prepare(col)
        for d in range(1, zn):
            for step in groups[d - 1]:
                target(step).start()

            @pl.when(z - d >= 0)
            def _():
                pass_up(d)

            @pl.when(z + d < zn)
            def _():
                pass_down(d)

            @pl.when(z - d >= 0)
            def _():
                prepare(col - d * xn)

            @pl.when(z + d < zn)
            def _():
                prepare(col + d * xn)

            if d < zn - 1:
                take_sides(d - 1)
        for step in groups[zn - 1]:
            target(step).start()

        @pl.when(row == 0)
        def _():
            remote(note, note, note_fwd.at[0], note_recv, (row, col)).wait_recv()
            for step in range(1, rows_n):
                note_on(step).start()

        take_sides(zn - 2)

        @pl.when(row > 0)
        def _():
            remote(note, note, note_fwd.at[0], note_recv, (row, col)).wait_recv()

    @pl.when(row == last)
    def _():
        ks[...] = gp[col]

    @pl.when(row != last)
    def _():
        remote(gp.at[col], ks, ks_send.at[0], ks_recv, (row, col)).wait_recv()

    inverse = note[:, size:]
    wide = jnp.concatenate([note[...]] * 4, axis=0).T[size:, :]
    high, mid, low = split3(wide)
    rhs[...] = jnp.concatenate([high, high, high, mid, low, mid], axis=0)
    pf_ref[...] = dot(inverse, gp[col], precision=HIGHEST)
    slab_factor = dot(inverse, ks[...], precision=HIGHEST)
    high, mid, _ = split3(slab_factor)
    yp[...] = jnp.concatenate([high, mid, high, mid], axis=0)
    solved = dot(note[:tgt, :size], wide, precision=HIGHEST)
    lanes = lax.broadcasted_iota(jnp.int32, solved.shape, 1)
    rest = solved - solved.astype(jnp.bfloat16).astype(jnp.float32)
    zp_ref[...] = jnp.where(lax.rem(lanes, 2 * size) < size, solved, rest).astype(jnp.bfloat16)
    z_ref[...] = solved[:, : 2 * size]
    sel_ref[...] = jnp.where((lanes[:, : 2 * size] < size) & (row == 0), 1.0, 0.0)

    lanes4 = lax.broadcasted_iota(jnp.int32, (blk, 4 * size), 1)

    def update(b):
        xt = dot(lhs[b], rhs[: 4 * size]) + dot(lhs[b, :, : 2 * size], rhs[4 * size :])
        rest = xt - xt.astype(jnp.bfloat16).astype(jnp.float32)
        packed = jnp.where(lanes4 < 2 * size, xt, rest).astype(jnp.bfloat16)
        xtp[b] = packed
        slab_copy(b).wait()
        part = pl.ds(pl.multiple_of(b * blk, blk), blk)
        us_ref[part, :] = us_ref[part, :] - dot(packed, yp[...])

    def update_step(b, carry):
        update(b)
        return carry

    take_sides(zn - 1)
    lax.fori_loop(0, cols_n, update_step, 0)

    @pl.when(row == 0)
    def _():
        us_ref[:size, :] = slab_factor

    own_target.wait()
    for step in range(1, cols_n):
        o = lax.rem(col + step, cols_n)
        remote(t_ref.at[pl.ds(0, tgt)], tg.at[o], t_send.at[0], t_recv.at[o], (row, col)).wait_recv()

    for zo in range(zn):
        for h in range(PIECES):
            @pl.when((z >= zo) & (z + 1 < zn))
            def _():
                up(zo, h).wait_send()

            @pl.when((z <= zo) & (z > 0))
            def _():
                down(zo, h).wait_send()

            for step in range(1, xn):
                side(zo, step, h).wait_send()

    for step in range(1, cols_n):
        target(step).wait_send()

    @pl.when(row == last)
    def _():
        for step in range(1, rows_n):
            slab_panel(step).wait_send()

    @pl.when(first_device)
    def _():
        for c in range(1, cols_n):
            note_out(c).wait_send()

    @pl.when(row == 0)
    def _():
        for step in range(1, rows_n):
            note_on(step).wait_send()


def finish(us_in, tg, xtp, pf_in, zp, z_in, sel, us_out, st_out, pf_out, st, sems):
    count, _, blk = tg.shape
    part_rows = us_in.shape[0] // 4
    copies = []
    for part in range(4):
        rows = pl.ds(part * part_rows, part_rows)
        copies.append(pltpu.make_async_copy(us_in.at[rows], us_out.at[rows], sems.at[part]))
    copies.append(pltpu.make_async_copy(pf_in, pf_out, sems.at[4]))
    for copy in copies:
        copy.start()
    for b in range(count):
        st[:, b * blk : (b + 1) * blk] = tg[b] - dot(zp[...], xtp[b], dims=((1,), (1,)))
    width = z_in.shape[1]
    st[:, :width] = jnp.where(sel[...] > 0.5, z_in[...], st[:, :width])
    copies.append(pltpu.make_async_copy(st, st_out, sems.at[5]))
    copies[-1].start()
    for copy in copies:
        copy.wait()


def body(rows_n, cols_n, kernel_panel, kernel_slab, targets):
    size, blk = kernel_panel.shape
    rows, _ = kernel_slab.shape
    tgt = targets.shape[0] // cols_n
    xn = cols_n // Z_SIZE
    f32, bf16 = jnp.float32, jnp.bfloat16
    hbm = pl.BlockSpec(memory_space=pltpu.HBM)
    vmem = pl.BlockSpec(memory_space=pltpu.VMEM)
    dma = pltpu.SemaphoreType.DMA
    held = pl.pallas_call(
        functools.partial(kernel, rows_n, cols_n),
        out_shape=[
            pltpu.VMEM((rows, blk), f32),
            pltpu.VMEM((cols_n, tgt, blk), f32),
            pltpu.VMEM((cols_n, blk, 4 * size), bf16),
            pltpu.VMEM((size, blk), f32),
            pltpu.VMEM((tgt, 4 * size), bf16),
            pltpu.VMEM((tgt, 2 * size), f32),
            pltpu.VMEM((tgt, 2 * size), f32),
        ],
        in_specs=[hbm] * 3,
        out_specs=[vmem] * 7,
        scratch_shapes=[
            pltpu.VMEM((cols_n, size, blk), f32),
            pltpu.VMEM((size, blk), f32),
            pltpu.VMEM((size, 2 * size), f32),
            pltpu.VMEM((cols_n, size, 2 * size), f32),
            pltpu.VMEM((cols_n * tgt, 2 * size), f32),
            pltpu.VMEM((cols_n, blk, 4 * size), bf16),
            pltpu.VMEM((6 * size, 4 * size), bf16),
            pltpu.VMEM((4 * size, blk), bf16),
            dma((cols_n,)), dma((3,)), dma((Z_SIZE, PIECES)), dma((Z_SIZE, PIECES)),
            dma((Z_SIZE, xn - 1, PIECES)), dma((cols_n, PIECES)),
            dma((cols_n - 1,)), dma((cols_n,)), dma((rows_n - 1,)), dma,
            dma((cols_n,)), dma((rows_n - 1,)), dma,
        ],
        compiler_params=pltpu.CompilerParams(
            collective_id=0, has_side_effects=True, vmem_limit_bytes=48 * 1024 * 1024
        ),
        cost_estimate=pl.CostEstimate(
            flops=2 * rows * blk * 4 * size, bytes_accessed=4 * rows * blk, transcendentals=0
        ),
    )(kernel_panel, targets, kernel_slab)
    return pl.pallas_call(
        finish,
        out_shape=[
            jax.ShapeDtypeStruct((rows, blk), f32),
            jax.ShapeDtypeStruct((tgt, rows), f32),
            jax.ShapeDtypeStruct((size, blk), f32),
        ],
        in_specs=[vmem] * 7,
        out_specs=[hbm] * 3,
        scratch_shapes=[pltpu.VMEM((tgt, rows), f32), dma((6,))],
        compiler_params=pltpu.CompilerParams(vmem_limit_bytes=36 * 1024 * 1024),
        cost_estimate=pl.CostEstimate(
            flops=2 * rows * tgt * 4 * size, bytes_accessed=4 * rows * blk, transcendentals=0
        ),
    )(*held)


def solution(mesh):
    in_specs = (P(None, ("row", "col")), P("row", "col"), P(None, ("row", "col")))
    out_specs = (P("row", "col"), P("col", "row"), P(None, ("row", "col")))
    step = functools.partial(body, mesh.shape["row"], mesh.shape["col"])
    return jax.shard_map(step, mesh=mesh, in_specs=in_specs, out_specs=out_specs, check_vma=False)
```

```python
import functools

import jax
import jax.numpy as jnp
from jax import lax
from jax.experimental import pallas as pl
from jax.experimental.pallas import tpu as pltpu
from jax.sharding import PartitionSpec as P

MESH = pl.DeviceIdType.MESH
HIGHEST = lax.Precision.HIGHEST
Z_SIZE = 4
PIECES = 2
EARLY = 16


def dot(a, b, dims=((1,), (0,)), precision=None):
    return lax.dot_general(a, b, (dims, ((), ())), precision=precision, preferred_element_type=jnp.float32)


def split3(value):
    high = value.astype(jnp.bfloat16)
    rest = value - high.astype(jnp.float32)
    mid = rest.astype(jnp.bfloat16)
    low = (rest - mid.astype(jnp.float32)).astype(jnp.bfloat16)
    return high, mid, low


def eliminate(work, begin, end):
    groups = [work[g : g + 8] for g in range(0, begin // 8 * 8, 8)]
    work = work[begin // 8 * 8 :]
    for j in range(begin, end, 2):
        i = j % 8
        rows = lax.broadcasted_iota(jnp.int32, work.shape, 0)
        first, second = work[i : i + 1, :], work[i + 1 : i + 2, :]
        cross = work[i + 1 : i + 2, j : j + 1]
        scale = 1.0 / work[i : i + 1, j : j + 1]
        ratio = cross * scale
        below = second - ratio * first
        other = 1.0 / (work[i + 1 : i + 2, j + 1 : j + 2] - ratio * cross)
        second_part = below * other
        first_part = first * scale - ratio * second_part
        change = work[:, j : j + 1] * first_part + work[:, j + 1 : j + 2] * second_part
        work = jnp.where(rows > i + 1, work - change, jnp.where(rows == i + 1, below, work))
        if i == 6:
            groups.append(work[:8])
            work = work[8:]
    return jnp.concatenate(groups + ([work] if end < groups[0].shape[1] // 2 else []), axis=0)


def kernel(
    rows_n, cols_n, k_ref, t_ref, s_ref,
    us_ref, tg, lhs, note, own_ref, sel_ref,
    gp, ks, notes, lead, weights,
    slab_sem, own_sem, up_sem, down_sem, side_sem, panel_sem, t_send, t_recv, ks_send, ks_recv,
    note_send, note_fwd, note_recv,
):
    row, col = lax.axis_index("row"), lax.axis_index("col")
    size, blk = k_ref.shape
    tgt = tg.shape[1]
    zn = Z_SIZE
    xn = cols_n // zn
    z, x = col // xn, col % xn
    last = rows_n - 1
    first_device = (row == 0) & (col == 0)

    def remote(src, dst, send, recv, where):
        return pltpu.make_async_remote_copy(
            src_ref=src, dst_ref=dst, send_sem=send, recv_sem=recv, device_id=where, device_id_type=MESH
        )

    def slab_copy(b):
        part = pl.ds(pl.multiple_of(b * blk, blk), blk)
        return pltpu.make_async_copy(s_ref.at[part], us_ref.at[part], slab_sem.at[b])

    own_panel = pltpu.make_async_copy(k_ref, gp.at[col], own_sem.at[0])
    own_target = pltpu.make_async_copy(
        t_ref.at[pl.ds(pl.multiple_of(col * tgt, tgt), tgt)], tg.at[col], own_sem.at[1]
    )
    own_lead = pltpu.make_async_copy(t_ref.at[:, pl.ds(0, 2 * size)], lead, own_sem.at[2])

    barrier = pltpu.get_barrier_semaphore()
    for step in range(1, cols_n):
        pl.semaphore_signal(barrier, inc=1, device_id=(row, lax.rem(col + step, cols_n)), device_id_type=MESH)
    for step in range(1, rows_n):
        pl.semaphore_signal(barrier, inc=1, device_id=(lax.rem(row + step, rows_n), col), device_id_type=MESH)
    own_panel.start()
    own_target.start()

    @pl.when(first_device)
    def _():
        own_lead.start()

    for b in range(cols_n):
        slab_copy(b).start()
    own_panel.wait()

    @pl.when(first_device)
    def _():
        corner = gp[0, :, : 2 * size]
        rows = lax.broadcasted_iota(jnp.int32, corner.shape, 0)
        lanes = lax.broadcasted_iota(jnp.int32, corner.shape, 1)
        work = jnp.where(lanes < size, corner, jnp.where(lanes == rows + size, 1.0, 0.0))
        notes[0] = eliminate(work, 0, EARLY)

    pl.semaphore_wait(barrier, cols_n - 1 + rows_n - 1)

    def piece(o, h):
        return gp.at[o, pl.ds(h * (size // PIECES), size // PIECES)]

    def up(zo, h):
        o = zo * xn + x
        return remote(piece(o, h), piece(o, h), up_sem.at[zo, h], panel_sem.at[o, h], (row, col + xn))

    def down(zo, h):
        o = zo * xn + x
        return remote(piece(o, h), piece(o, h), down_sem.at[zo, h], panel_sem.at[o, h], (row, col - xn))

    def side(zo, step, h):
        o = zo * xn + x
        peer = z * xn + lax.rem(x + step, xn)
        return remote(piece(o, h), piece(o, h), side_sem.at[zo, step - 1, h], panel_sem.at[o, h], (row, peer))

    def slab_panel(step):
        return remote(gp.at[col], ks, ks_send.at[step - 1], ks_recv, (lax.rem(row + step, rows_n), col))

    def target(step):
        peer = lax.rem(col + step, cols_n)
        return remote(
            t_ref.at[pl.ds(pl.multiple_of(peer * tgt, tgt), tgt)], tg.at[col],
            t_send.at[step - 1], t_recv.at[col], (row, peer),
        )

    def note_out(c):
        return remote(notes.at[c], note, note_send.at[c], note_recv, (row, c))

    def note_on(step):
        return remote(note, note, note_fwd.at[step - 1], note_recv, (lax.rem(row + step, rows_n), col))

    half = lax.broadcasted_iota(jnp.int32, (blk, 2 * size), 1) < size

    def prepare(o):
        block = gp[o]
        turned = jnp.concatenate([block, block], axis=0).T
        high = turned.astype(jnp.bfloat16).astype(jnp.float32)
        rest = turned - high
        mid = rest.astype(jnp.bfloat16).astype(jnp.float32)
        pair = jnp.where(half, high, mid).astype(jnp.bfloat16)
        other = jnp.where(half, rest - mid, high).astype(jnp.bfloat16)
        lhs[o] = jnp.concatenate([pair, other], axis=1)

    def pass_up(d):
        for h in range(PIECES):
            up(z - d, h).wait_recv()

            @pl.when(z + 1 < zn)
            def _():
                up(z - d, h).start()

            for step in range(1, xn):
                side(z - d, step, h).start()

    def pass_down(d):
        for h in range(PIECES):
            down(z + d, h).wait_recv()

            @pl.when(z > 0)
            def _():
                down(z + d, h).start()

            for step in range(1, xn):
                side(z + d, step, h).start()

    def take_side(zo):
        for step in range(1, xn):
            o = zo * xn + lax.rem(x + step, xn)
            for h in range(PIECES):
                remote(piece(o, h), piece(o, h), side_sem.at[0, 0, 0], panel_sem.at[o, h], (row, col)).wait_recv()
            prepare(o)

    def take_sides(d):
        if d == 0:
            take_side(z)
        else:
            @pl.when(z - d >= 0)
            def _():
                take_side(z - d)

            @pl.when(z + d < zn)
            def _():
                take_side(z + d)

    for h in range(PIECES):
        @pl.when(z + 1 < zn)
        def _():
            up(z, h).start()

        @pl.when(z > 0)
        def _():
            down(z, h).start()

        for step in range(1, xn):
            side(z, step, h).start()

    @pl.when(row == last)
    def _():
        for step in range(1, rows_n):
            slab_panel(step).start()

    sends = list(range(1, cols_n))
    groups = [sends[g::zn] for g in range(zn)]

    @pl.when(first_device)
    def _():
        for step in sends:
            target(step).start()
        work = eliminate(notes[0], EARLY, size)
        rows = lax.broadcasted_iota(jnp.int32, work.shape, 0)
        lanes = lax.broadcasted_iota(jnp.int32, work.shape, 1)
        diagonal = jnp.sum(jnp.where(lanes == rows, work, 0.0), axis=1, keepdims=True)
        done = work * (1.0 / jnp.sqrt(diagonal))
        own_lead.wait()
        for c in range(cols_n):
            notes[c] = done
            notes[c, :tgt, :] = jnp.where(lanes[:tgt] < size, lead[c * tgt : (c + 1) * tgt, :], done[:tgt])
        for c in range(1, cols_n):
            note_out(c).start()
        note[...] = notes[0]
        for step in range(1, rows_n):
            note_on(step).start()
        for d in range(1, zn):
            pass_down(d)
        prepare(col)
        for d in range(1, zn):
            prepare(col + d * xn)
            take_sides(d - 1)

    @pl.when(jnp.logical_not(first_device))
    def _():
        prepare(col)
        for d in range(1, zn):
            for step in groups[d - 1]:
                target(step).start()

            @pl.when(z - d >= 0)
            def _():
                pass_up(d)

            @pl.when(z + d < zn)
            def _():
                pass_down(d)

            @pl.when(z - d >= 0)
            def _():
                prepare(col - d * xn)

            @pl.when(z + d < zn)
            def _():
                prepare(col + d * xn)

            if d < zn - 1:
                take_sides(d - 1)
        for step in groups[zn - 1]:
            target(step).start()

        @pl.when(row == 0)
        def _():
            remote(note, note, note_fwd.at[0], note_recv, (row, col)).wait_recv()
            for step in range(1, rows_n):
                note_on(step).start()

        take_sides(zn - 2)

        @pl.when(row > 0)
        def _():
            remote(note, note, note_fwd.at[0], note_recv, (row, col)).wait_recv()

    @pl.when(row == last)
    def _():
        ks[...] = gp[col]

    @pl.when(row != last)
    def _():
        remote(gp.at[col], ks, ks_send.at[0], ks_recv, (row, col)).wait_recv()

    own_ref[...] = gp[col]
    lanes = lax.broadcasted_iota(jnp.int32, sel_ref.shape, 1)
    sel_ref[...] = jnp.where((lanes < size) & (row == 0), 1.0, 0.0)
    slab_factor = dot(note[:, size:], ks[...], precision=HIGHEST)
    turned = jnp.concatenate([note[...]] * 2, axis=0).T[size:, :size]
    high, mid, low = split3(dot(turned, slab_factor, precision=HIGHEST))
    weights[...] = jnp.concatenate([high, high, high, mid, low, mid], axis=0)
    for b in range(cols_n):
        slab_copy(b).wait()

    take_sides(zn - 1)
    for b in range(cols_n):
        part = slice(b * blk, (b + 1) * blk)
        product = dot(lhs[b], weights[: 4 * size]) + dot(lhs[b, :, : 2 * size], weights[4 * size :])
        us_ref[part, :] = us_ref[part, :] - product

    @pl.when(row == 0)
    def _():
        us_ref[:size, :] = slab_factor

    own_target.wait()
    for step in range(1, cols_n):
        o = lax.rem(col + step, cols_n)
        remote(t_ref.at[pl.ds(0, tgt)], tg.at[o], t_send.at[0], t_recv.at[o], (row, col)).wait_recv()

    for zo in range(zn):
        for h in range(PIECES):
            @pl.when((z >= zo) & (z + 1 < zn))
            def _():
                up(zo, h).wait_send()

            @pl.when((z <= zo) & (z > 0))
            def _():
                down(zo, h).wait_send()

            for step in range(1, xn):
                side(zo, step, h).wait_send()

    for step in range(1, cols_n):
        target(step).wait_send()

    @pl.when(row == last)
    def _():
        for step in range(1, rows_n):
            slab_panel(step).wait_send()

    @pl.when(first_device)
    def _():
        for c in range(1, cols_n):
            note_out(c).wait_send()

    @pl.when(row == 0)
    def _():
        for step in range(1, rows_n):
            note_on(step).wait_send()


def finish(us_in, tg, lhs, note, own, sel, us_out, st_out, pf_out, st, pf, sems):
    count, tgt, blk = tg.shape
    size = own.shape[0]
    part_rows = us_in.shape[0] // 4
    copies = []
    for part in range(4):
        rows = pl.ds(part * part_rows, part_rows)
        copies.append(pltpu.make_async_copy(us_in.at[rows], us_out.at[rows], sems.at[part]))
    for copy in copies:
        copy.start()
    inverse = note[:, size:]
    pf[...] = dot(inverse, own[...], precision=HIGHEST)
    copies.append(pltpu.make_async_copy(pf, pf_out, sems.at[4]))
    copies[-1].start()
    solved = dot(note[:tgt, :size], inverse, dims=((1,), (1,)), precision=HIGHEST)
    repeated = jnp.concatenate([inverse] * 4, axis=1)
    high, mid, low = (v.astype(jnp.float32) for v in split3(dot(solved, repeated, precision=HIGHEST)))
    lanes = lax.broadcasted_iota(jnp.int32, high.shape, 1)
    front = jnp.where(lanes < 3 * size, high, mid).astype(jnp.bfloat16)
    back = jnp.where(lanes < size, low, mid)[:, : 2 * size].astype(jnp.bfloat16)
    for b in range(count):
        product = dot(front, lhs[b], dims=((1,), (1,))) + dot(back, lhs[b, :, : 2 * size], dims=((1,), (1,)))
        st[:, b * blk : (b + 1) * blk] = tg[b] - product
    st[:, :size] = jnp.where(sel[:, :size] > 0.5, solved, st[:, :size])
    copies.append(pltpu.make_async_copy(st, st_out, sems.at[5]))
    copies[-1].start()
    for copy in copies:
        copy.wait()


def body(rows_n, cols_n, kernel_panel, kernel_slab, targets):
    size, blk = kernel_panel.shape
    rows, _ = kernel_slab.shape
    tgt = targets.shape[0] // cols_n
    xn = cols_n // Z_SIZE
    f32, bf16 = jnp.float32, jnp.bfloat16
    hbm = pl.BlockSpec(memory_space=pltpu.HBM)
    vmem = pl.BlockSpec(memory_space=pltpu.VMEM)
    dma = pltpu.SemaphoreType.DMA
    held = pl.pallas_call(
        functools.partial(kernel, rows_n, cols_n),
        out_shape=[
            pltpu.VMEM((rows, blk), f32),
            pltpu.VMEM((cols_n, tgt, blk), f32),
            pltpu.VMEM((cols_n, blk, 4 * size), bf16),
            pltpu.VMEM((size, 2 * size), f32),
            pltpu.VMEM((size, blk), f32),
            pltpu.VMEM((tgt, 2 * size), f32),
        ],
        in_specs=[hbm] * 3,
        out_specs=[vmem] * 6,
        scratch_shapes=[
            pltpu.VMEM((cols_n, size, blk), f32),
            pltpu.VMEM((size, blk), f32),
            pltpu.VMEM((cols_n, size, 2 * size), f32),
            pltpu.VMEM((cols_n * tgt, 2 * size), f32),
            pltpu.VMEM((6 * size, blk), bf16),
            dma((cols_n,)), dma((3,)), dma((Z_SIZE, PIECES)), dma((Z_SIZE, PIECES)),
            dma((Z_SIZE, xn - 1, PIECES)), dma((cols_n, PIECES)),
            dma((cols_n - 1,)), dma((cols_n,)), dma((rows_n - 1,)), dma,
            dma((cols_n,)), dma((rows_n - 1,)), dma,
        ],
        compiler_params=pltpu.CompilerParams(
            collective_id=0, has_side_effects=True, vmem_limit_bytes=48 * 1024 * 1024
        ),
        cost_estimate=pl.CostEstimate(
            flops=2 * rows * blk * 6 * size, bytes_accessed=4 * rows * blk, transcendentals=0
        ),
    )(kernel_panel, targets, kernel_slab)
    return pl.pallas_call(
        finish,
        out_shape=[
            jax.ShapeDtypeStruct((rows, blk), f32),
            jax.ShapeDtypeStruct((tgt, rows), f32),
            jax.ShapeDtypeStruct((size, blk), f32),
        ],
        in_specs=[vmem] * 6,
        out_specs=[hbm] * 3,
        scratch_shapes=[pltpu.VMEM((tgt, rows), f32), pltpu.VMEM((size, blk), f32), dma((6,))],
        compiler_params=pltpu.CompilerParams(vmem_limit_bytes=36 * 1024 * 1024),
        cost_estimate=pl.CostEstimate(
            flops=2 * rows * tgt * 4 * size, bytes_accessed=4 * rows * blk, transcendentals=0
        ),
    )(*held)


def solution(mesh):
    in_specs = (P(None, ("row", "col")), P("row", "col"), P(None, ("row", "col")))
    out_specs = (P("row", "col"), P("col", "row"), P(None, ("row", "col")))
    step = functools.partial(body, mesh.shape["row"], mesh.shape["col"])
    return jax.shard_map(step, mesh=mesh, in_specs=in_specs, out_specs=out_specs, check_vma=False)
```

```python
import functools

import jax
import jax.numpy as jnp
from jax import lax
from jax.experimental import pallas as pl
from jax.experimental.pallas import tpu as pltpu
from jax.sharding import PartitionSpec as P

MESH = pl.DeviceIdType.MESH
HIGHEST = lax.Precision.HIGHEST
Z_SIZE = 4
PIECES = 2
EARLY = 40


def dot(a, b, dims=((1,), (0,)), precision=None):
    return lax.dot_general(a, b, (dims, ((), ())), precision=precision, preferred_element_type=jnp.float32)


def split3(value):
    high = value.astype(jnp.bfloat16)
    rest = value - high.astype(jnp.float32)
    mid = rest.astype(jnp.bfloat16)
    low = (rest - mid.astype(jnp.float32)).astype(jnp.bfloat16)
    return high, mid, low


def eliminate(work, begin, end):
    groups = [work[g : g + 8] for g in range(0, begin // 8 * 8, 8)]
    work = work[begin // 8 * 8 :]
    for j in range(begin, end, 2):
        i = j % 8
        rows = lax.broadcasted_iota(jnp.int32, work.shape, 0)
        first, second = work[i : i + 1, :], work[i + 1 : i + 2, :]
        cross = work[i + 1 : i + 2, j : j + 1]
        scale = 1.0 / work[i : i + 1, j : j + 1]
        ratio = cross * scale
        below = second - ratio * first
        other = 1.0 / (work[i + 1 : i + 2, j + 1 : j + 2] - ratio * cross)
        second_part = below * other
        first_part = first * scale - ratio * second_part
        change = work[:, j : j + 1] * first_part + work[:, j + 1 : j + 2] * second_part
        work = jnp.where(rows > i + 1, work - change, jnp.where(rows == i + 1, below, work))
        if i == 6:
            groups.append(work[:8])
            work = work[8:]
    return jnp.concatenate(groups + ([work] if end < groups[0].shape[1] // 2 else []), axis=0)


def kernel(
    rows_n, cols_n, k_ref, t_ref, s_ref,
    us_ref, tg, lhs, note, own_ref, sel_ref,
    gp, ks, notes, lead, weights,
    slab_sem, own_sem, up_sem, down_sem, side_sem, panel_sem, t_send, t_recv, ks_send, ks_recv,
    note_send, note_fwd, note_recv,
):
    row, col = lax.axis_index("row"), lax.axis_index("col")
    size, blk = k_ref.shape
    tgt = tg.shape[1]
    zn = Z_SIZE
    xn = cols_n // zn
    z, x = col // xn, col % xn
    last = rows_n - 1
    first_device = (row == 0) & (col == 0)

    def remote(src, dst, send, recv, where):
        return pltpu.make_async_remote_copy(
            src_ref=src, dst_ref=dst, send_sem=send, recv_sem=recv, device_id=where, device_id_type=MESH
        )

    def slab_copy(b):
        part = pl.ds(pl.multiple_of(b * blk, blk), blk)
        return pltpu.make_async_copy(s_ref.at[part], us_ref.at[part], slab_sem.at[b])

    own_panel = pltpu.make_async_copy(k_ref, gp.at[col], own_sem.at[0])
    own_target = pltpu.make_async_copy(
        t_ref.at[pl.ds(pl.multiple_of(col * tgt, tgt), tgt)], tg.at[col], own_sem.at[1]
    )
    own_lead = pltpu.make_async_copy(t_ref.at[:, pl.ds(0, 2 * size)], lead, own_sem.at[2])

    barrier = pltpu.get_barrier_semaphore()
    for step in range(1, cols_n):
        pl.semaphore_signal(barrier, inc=1, device_id=(row, lax.rem(col + step, cols_n)), device_id_type=MESH)
    for step in range(1, rows_n):
        pl.semaphore_signal(barrier, inc=1, device_id=(lax.rem(row + step, rows_n), col), device_id_type=MESH)
    own_panel.start()
    own_target.start()

    @pl.when(first_device)
    def _():
        own_lead.start()

    for b in range(cols_n):
        slab_copy(b).start()
    own_panel.wait()

    @pl.when(first_device)
    def _():
        corner = gp[0, :, : 2 * size]
        rows = lax.broadcasted_iota(jnp.int32, corner.shape, 0)
        lanes = lax.broadcasted_iota(jnp.int32, corner.shape, 1)
        work = jnp.where(lanes < size, corner, jnp.where(lanes == rows + size, 1.0, 0.0))
        notes[0] = eliminate(work, 0, EARLY)

    pl.semaphore_wait(barrier, cols_n - 1 + rows_n - 1)

    def piece(o, h):
        return gp.at[o, pl.ds(h * (size // PIECES), size // PIECES)]

    def up(zo, h):
        o = zo * xn + x
        return remote(piece(o, h), piece(o, h), up_sem.at[zo, h], panel_sem.at[o, h], (row, col + xn))

    def down(zo, h):
        o = zo * xn + x
        return remote(piece(o, h), piece(o, h), down_sem.at[zo, h], panel_sem.at[o, h], (row, col - xn))

    def side(zo, step, h):
        o = zo * xn + x
        peer = z * xn + lax.rem(x + step, xn)
        return remote(piece(o, h), piece(o, h), side_sem.at[zo, step - 1, h], panel_sem.at[o, h], (row, peer))

    def slab_panel(step):
        return remote(gp.at[col], ks, ks_send.at[step - 1], ks_recv, (lax.rem(row + step, rows_n), col))

    def target(step):
        peer = lax.rem(col + step, cols_n)
        return remote(
            t_ref.at[pl.ds(pl.multiple_of(peer * tgt, tgt), tgt)], tg.at[col],
            t_send.at[step - 1], t_recv.at[col], (row, peer),
        )

    def note_out(c):
        return remote(notes.at[c], note, note_send.at[c], note_recv, (row, c))

    def note_on(step):
        return remote(note, note, note_fwd.at[step - 1], note_recv, (lax.rem(row + step, rows_n), col))

    half = lax.broadcasted_iota(jnp.int32, (blk, 2 * size), 1) < size

    def prepare(o):
        block = gp[o]
        turned = jnp.concatenate([block, block], axis=0).T
        high = turned.astype(jnp.bfloat16).astype(jnp.float32)
        rest = turned - high
        mid = rest.astype(jnp.bfloat16).astype(jnp.float32)
        pair = jnp.where(half, high, mid).astype(jnp.bfloat16)
        other = jnp.where(half, rest - mid, high).astype(jnp.bfloat16)
        lhs[o] = jnp.concatenate([pair, other], axis=1)

    def pass_up(d):
        for h in range(PIECES):
            up(z - d, h).wait_recv()

            @pl.when(z + 1 < zn)
            def _():
                up(z - d, h).start()

            for step in range(1, xn):
                side(z - d, step, h).start()

    def pass_down(d):
        for h in range(PIECES):
            down(z + d, h).wait_recv()

            @pl.when(z > 0)
            def _():
                down(z + d, h).start()

            for step in range(1, xn):
                side(z + d, step, h).start()

    def take_side(zo):
        for step in range(1, xn):
            o = zo * xn + lax.rem(x + step, xn)
            for h in range(PIECES):
                remote(piece(o, h), piece(o, h), side_sem.at[0, 0, 0], panel_sem.at[o, h], (row, col)).wait_recv()
            prepare(o)

    def take_sides(d):
        if d == 0:
            take_side(z)
        else:
            @pl.when(z - d >= 0)
            def _():
                take_side(z - d)

            @pl.when(z + d < zn)
            def _():
                take_side(z + d)

    for h in range(PIECES):
        @pl.when(z + 1 < zn)
        def _():
            up(z, h).start()

        @pl.when(z > 0)
        def _():
            down(z, h).start()

        for step in range(1, xn):
            side(z, step, h).start()

    @pl.when(row == last)
    def _():
        for step in range(1, rows_n):
            slab_panel(step).start()

    sends = list(range(1, cols_n))
    groups = [sends[g::zn] for g in range(zn)]

    @pl.when(first_device)
    def _():
        work = eliminate(notes[0], EARLY, size)
        rows = lax.broadcasted_iota(jnp.int32, work.shape, 0)
        lanes = lax.broadcasted_iota(jnp.int32, work.shape, 1)
        diagonal = jnp.sum(jnp.where(lanes == rows, work, 0.0), axis=1, keepdims=True)
        done = work * (1.0 / jnp.sqrt(diagonal))
        own_lead.wait()
        for c in range(cols_n):
            notes[c] = done
            notes[c, :tgt, :] = jnp.where(lanes[:tgt] < size, lead[c * tgt : (c + 1) * tgt, :], done[:tgt])
        for c in range(1, cols_n):
            note_out(c).start()
        note[...] = notes[0]
        for step in range(1, rows_n):
            note_on(step).start()
        for d in range(1, zn):
            pass_down(d)
        for step in sends:
            target(step).start()
        prepare(col)
        for d in range(1, zn):
            prepare(col + d * xn)
            take_sides(d - 1)

    @pl.when(jnp.logical_not(first_device))
    def _():
        prepare(col)
        for d in range(1, zn):
            for step in groups[d - 1]:
                target(step).start()

            @pl.when(z - d >= 0)
            def _():
                pass_up(d)

            @pl.when(z + d < zn)
            def _():
                pass_down(d)

            @pl.when(z - d >= 0)
            def _():
                prepare(col - d * xn)

            @pl.when(z + d < zn)
            def _():
                prepare(col + d * xn)

            if d < zn - 1:
                take_sides(d - 1)
        for step in groups[zn - 1]:
            target(step).start()

        @pl.when(row == 0)
        def _():
            remote(note, note, note_fwd.at[0], note_recv, (row, col)).wait_recv()
            for step in range(1, rows_n):
                note_on(step).start()

        take_sides(zn - 2)

        @pl.when(row > 0)
        def _():
            remote(note, note, note_fwd.at[0], note_recv, (row, col)).wait_recv()

    @pl.when(row == last)
    def _():
        ks[...] = gp[col]

    @pl.when(row != last)
    def _():
        remote(gp.at[col], ks, ks_send.at[0], ks_recv, (row, col)).wait_recv()

    own_ref[...] = gp[col]
    lanes = lax.broadcasted_iota(jnp.int32, sel_ref.shape, 1)
    sel_ref[...] = jnp.where((lanes < size) & (row == 0), 1.0, 0.0)
    slab_factor = dot(note[:, size:], ks[...], precision=HIGHEST)
    turned = jnp.concatenate([note[...]] * 2, axis=0).T[size:, :size]
    high, mid, low = split3(dot(turned, slab_factor, precision=HIGHEST))
    weights[...] = jnp.concatenate([high, high, high, mid, low, mid], axis=0)
    for b in range(cols_n):
        slab_copy(b).wait()

    take_sides(zn - 1)
    for b in range(cols_n):
        part = slice(b * blk, (b + 1) * blk)
        product = dot(lhs[b], weights[: 4 * size]) + dot(lhs[b, :, : 2 * size], weights[4 * size :])
        us_ref[part, :] = us_ref[part, :] - product

    @pl.when(row == 0)
    def _():
        us_ref[:size, :] = slab_factor

    own_target.wait()
    for step in range(1, cols_n):
        o = lax.rem(col + step, cols_n)
        remote(t_ref.at[pl.ds(0, tgt)], tg.at[o], t_send.at[0], t_recv.at[o], (row, col)).wait_recv()

    for zo in range(zn):
        for h in range(PIECES):
            @pl.when((z >= zo) & (z + 1 < zn))
            def _():
                up(zo, h).wait_send()

            @pl.when((z <= zo) & (z > 0))
            def _():
                down(zo, h).wait_send()

            for step in range(1, xn):
                side(zo, step, h).wait_send()

    for step in range(1, cols_n):
        target(step).wait_send()

    @pl.when(row == last)
    def _():
        for step in range(1, rows_n):
            slab_panel(step).wait_send()

    @pl.when(first_device)
    def _():
        for c in range(1, cols_n):
            note_out(c).wait_send()

    @pl.when(row == 0)
    def _():
        for step in range(1, rows_n):
            note_on(step).wait_send()


def finish(us_in, tg, lhs, note, own, sel, us_out, st_out, pf_out, st, pf, sems):
    count, tgt, blk = tg.shape
    size = own.shape[0]
    part_rows = us_in.shape[0] // 4
    copies = []
    for part in range(4):
        rows = pl.ds(part * part_rows, part_rows)
        copies.append(pltpu.make_async_copy(us_in.at[rows], us_out.at[rows], sems.at[part]))
    for copy in copies:
        copy.start()
    inverse = note[:, size:]
    pf[...] = dot(inverse, own[...], precision=HIGHEST)
    copies.append(pltpu.make_async_copy(pf, pf_out, sems.at[4]))
    copies[-1].start()
    solved = dot(note[:tgt, :size], inverse, dims=((1,), (1,)), precision=HIGHEST)
    repeated = jnp.concatenate([inverse] * 4, axis=1)
    high, mid, low = (v.astype(jnp.float32) for v in split3(dot(solved, repeated, precision=HIGHEST)))
    lanes = lax.broadcasted_iota(jnp.int32, high.shape, 1)
    front = jnp.where(lanes < 3 * size, high, mid).astype(jnp.bfloat16)
    back = jnp.where(lanes < size, low, mid)[:, : 2 * size].astype(jnp.bfloat16)
    for b in range(count):
        product = dot(front, lhs[b], dims=((1,), (1,))) + dot(back, lhs[b, :, : 2 * size], dims=((1,), (1,)))
        st[:, b * blk : (b + 1) * blk] = tg[b] - product
    st[:, :size] = jnp.where(sel[:, :size] > 0.5, solved, st[:, :size])
    copies.append(pltpu.make_async_copy(st, st_out, sems.at[5]))
    copies[-1].start()
    for copy in copies:
        copy.wait()


def body(rows_n, cols_n, kernel_panel, kernel_slab, targets):
    size, blk = kernel_panel.shape
    rows, _ = kernel_slab.shape
    tgt = targets.shape[0] // cols_n
    xn = cols_n // Z_SIZE
    f32, bf16 = jnp.float32, jnp.bfloat16
    hbm = pl.BlockSpec(memory_space=pltpu.HBM)
    vmem = pl.BlockSpec(memory_space=pltpu.VMEM)
    dma = pltpu.SemaphoreType.DMA
    held = pl.pallas_call(
        functools.partial(kernel, rows_n, cols_n),
        out_shape=[
            pltpu.VMEM((rows, blk), f32),
            pltpu.VMEM((cols_n, tgt, blk), f32),
            pltpu.VMEM((cols_n, blk, 4 * size), bf16),
            pltpu.VMEM((size, 2 * size), f32),
            pltpu.VMEM((size, blk), f32),
            pltpu.VMEM((tgt, 2 * size), f32),
        ],
        in_specs=[hbm] * 3,
        out_specs=[vmem] * 6,
        scratch_shapes=[
            pltpu.VMEM((cols_n, size, blk), f32),
            pltpu.VMEM((size, blk), f32),
            pltpu.VMEM((cols_n, size, 2 * size), f32),
            pltpu.VMEM((cols_n * tgt, 2 * size), f32),
            pltpu.VMEM((6 * size, blk), bf16),
            dma((cols_n,)), dma((3,)), dma((Z_SIZE, PIECES)), dma((Z_SIZE, PIECES)),
            dma((Z_SIZE, xn - 1, PIECES)), dma((cols_n, PIECES)),
            dma((cols_n - 1,)), dma((cols_n,)), dma((rows_n - 1,)), dma,
            dma((cols_n,)), dma((rows_n - 1,)), dma,
        ],
        compiler_params=pltpu.CompilerParams(
            collective_id=0, has_side_effects=True, vmem_limit_bytes=48 * 1024 * 1024
        ),
        cost_estimate=pl.CostEstimate(
            flops=2 * rows * blk * 6 * size, bytes_accessed=4 * rows * blk, transcendentals=0
        ),
    )(kernel_panel, targets, kernel_slab)
    return pl.pallas_call(
        finish,
        out_shape=[
            jax.ShapeDtypeStruct((rows, blk), f32),
            jax.ShapeDtypeStruct((tgt, rows), f32),
            jax.ShapeDtypeStruct((size, blk), f32),
        ],
        in_specs=[vmem] * 6,
        out_specs=[hbm] * 3,
        scratch_shapes=[pltpu.VMEM((tgt, rows), f32), pltpu.VMEM((size, blk), f32), dma((6,))],
        compiler_params=pltpu.CompilerParams(vmem_limit_bytes=36 * 1024 * 1024),
        cost_estimate=pl.CostEstimate(
            flops=2 * rows * tgt * 4 * size, bytes_accessed=4 * rows * blk, transcendentals=0
        ),
    )(*held)


def solution(mesh):
    in_specs = (P(None, ("row", "col")), P("row", "col"), P(None, ("row", "col")))
    out_specs = (P("row", "col"), P("col", "row"), P(None, ("row", "col")))
    step = functools.partial(body, mesh.shape["row"], mesh.shape["col"])
    return jax.shard_map(step, mesh=mesh, in_specs=in_specs, out_specs=out_specs, check_vma=False)
```
